256 devices in a mesh: sec: 2 (over core), tok: 8 (over x, y_lo), voc: 16 (over y_hi, z).
Axes of the slice: x: 4, y: 4 (y_hi: 2, y_lo: 2; y = y_hi * 2 + y_lo), z: 8, core: 2. Of those that a mesh axis runs over, the one named last changes fastest.
Arguments:
- context: bfloat16 [512, 2048], P(('sec', 'tok'), 'voc'), may hold values from -6 to 6
- residual_in: bfloat16 [512, 4608], P(('sec', 'tok'), 'voc'), may hold values from -6 to 6
- out_proj: bfloat16 [2048, 4608], P('voc'), may hold values from -0.125 to 0.125
- post_gain: float32 [4608], P('voc'), may hold values from 0.25 to 1.75
- final_gain: float32 [4608], P('voc'), may hold values from 0.25 to 1.75
- teacher_head: bfloat16 [131072, 4608], P(('sec', 'tok', 'voc')), may hold values from -0.25 to 0.25
- student_hidden: bfloat16 [512, 3584], P(('sec', 'tok'), 'voc'), may hold values from -6 to 6
- student_gain: float32 [3584], replicated, may hold values from 0.25 to 1.75
- student_head: bfloat16 [131072, 3584], P(('sec', 'tok', 'voc')), may hold values from -0.3125 to 0.3125
- kl_weight: float32 [512], replicated, may hold values from 20 to 200
Outputs:
- token_kl: float32 [512], P(('sec', 'tok', 'voc'))
- grad_hidden: bfloat16 [512, 3584], P(('sec', 'tok'), 'voc')
- grad_head: bfloat16 [131072, 3584], P(('sec', 'tok', 'voc'))
The draws below stay inside these ranges and needn't reach their ends.
All inputs are finite; a program needn't handle non-finite values.
Results may differ from the reference program's by a relative error of at most 0.014.
Values may be sent and summed in bfloat16 or wider, within the bound.
No kernel may reach another device: no remote copies, remote signals or barrier semaphores. Data moves between devices by JAX's collectives and lax.ppermute only.
A program may use at most 128 MiB of HBM per device.

```python
import math
import jax
import jax.numpy as jnp
from jax import lax

DT = 4608
DS = 3584
CTX = 2048
VOC_DEV = 512
TOKENS = 512
VOCAB = 131072


def shard_levels(rng, extent, shards, least, high):
    def one(position, shards_of):
        steps = jax.random.uniform(jax.random.fold_in(jax.random.fold_in(rng, 6), position), (shards_of,), jnp.float32, least / len(shards), high / len(shards))
        return jnp.repeat(jnp.exp(steps), extent[position] // shards_of).reshape((-1,) + (1,) * (len(extent) - position - 1))

    gain = one(*shards[0])
    for cut in shards[1:]:
        gain = gain * one(*cut)
    return gain


def scatter_about(stream_key, dims, deviation, limit, split=(), dtype=jnp.bfloat16):
    level = shard_levels(stream_key, dims, split, -0.22, 0.18) if split else 1.0
    result = jax.random.normal(stream_key, dims, jnp.float32) * deviation * level
    return jnp.minimum(jnp.maximum(result, -limit), limit).astype(dtype)


def setup_inputs(seed: int = 0) -> dict:
    streams_of = jax.random.split(jax.random.key(seed), 11)
    context = scatter_about(streams_of[0], (TOKENS, CTX), 1.0, 6.0, ((0, 16), (1, 16)))
    residual_in = scatter_about(streams_of[1], (TOKENS, DT), 1.0, 6.0, ((0, 16), (1, 16)))
    out_proj = scatter_about(streams_of[2], (CTX, DT), CTX ** -0.5, 0.125, ((0, 16),))
    post_gain = jnp.clip(1.0 + 0.15 * jax.random.normal(streams_of[3], (DT,), jnp.float32), 0.25, 1.75)
    final_gain = jnp.clip(1.0 + 0.15 * jax.random.normal(streams_of[4], (DT,), jnp.float32), 0.25, 1.75)
    teacher_head = scatter_about(streams_of[5], (VOCAB, DT), (DT // 9) ** -0.5, 0.25, ((0, 256),))
    student_hidden = scatter_about(streams_of[6], (TOKENS, DS), 1.0, 6.0, ((0, 16), (1, 16)))
    student_gain = jnp.clip(1.0 + 0.15 * jax.random.normal(streams_of[7], (DS,), jnp.float32), 0.25, 1.75)
    student_head = scatter_about(streams_of[8], (VOCAB, DS), (DS // 9) ** -0.5, 0.3125, ((0, 256),))
    kl_weight = jnp.clip(jnp.exp(jax.random.uniform(streams_of[9], (TOKENS,), jnp.float32, math.log(20.0), math.log(200.0))), 20.0, 200.0)
    return dict(context=context, residual_in=residual_in, out_proj=out_proj, post_gain=post_gain, final_gain=final_gain, teacher_head=teacher_head, student_hidden=student_hidden, student_gain=student_gain, student_head=student_head, kl_weight=kl_weight)


epsilon = 1e-06
softcap = 30.0

def reference(context, residual_in, out_proj, post_gain, final_gain, teacher_head, student_hidden, student_gain, student_head, kl_weight):
    attention = jnp.dot(context, out_proj, preferred_element_type=jnp.float32)
    post_scale = lax.rsqrt(lax.optimization_barrier(jnp.mean(attention * attention, axis=1, keepdims=True)) + epsilon)
    hidden = residual_in.astype(jnp.float32) + attention * post_scale * post_gain
    final_scale = lax.rsqrt(lax.optimization_barrier(jnp.mean(hidden * hidden, axis=1, keepdims=True)) + epsilon)
    teacher_normed = (hidden * final_scale * final_gain).astype(jnp.bfloat16)
    raw_student = student_hidden.astype(jnp.float32)
    student_scale = lax.rsqrt(lax.optimization_barrier(jnp.mean(raw_student * raw_student, axis=1, keepdims=True)) + epsilon)
    student_normed = (raw_student * student_scale * student_gain).astype(jnp.bfloat16)
    teacher_blocks = teacher_head.reshape(-1, VOC_DEV, DT)
    student_blocks = student_head.reshape(-1, VOC_DEV, DS)

    def logits(teacher_rows, student_rows):
        teacher_raw = jnp.dot(teacher_normed, teacher_rows.T, preferred_element_type=jnp.float32)
        student_raw = jnp.dot(student_normed, student_rows.T, preferred_element_type=jnp.float32)
        return (softcap * jnp.tanh(teacher_raw / softcap), jnp.tanh(student_raw / softcap))

    def first_pass(totals, pairs):
        teacher_logit, student_tanh = logits(pairs[0], pairs[1])
        student_logit = softcap * student_tanh
        teacher_exp = jnp.exp(teacher_logit)
        return ((totals[0] + lax.optimization_barrier(jnp.sum(teacher_exp, axis=1)), totals[1] + lax.optimization_barrier(jnp.sum(jnp.exp(student_logit), axis=1)), totals[2] + lax.optimization_barrier(jnp.sum(teacher_exp * (teacher_logit - student_logit), axis=1))), None)
    empty = jnp.zeros((TOKENS,), jnp.float32)
    sums, unused = lax.scan(first_pass, (empty, empty, empty), (teacher_blocks, student_blocks))
    teacher_total, student_total, mixed = sums
    token_kl = mixed / teacher_total + jnp.log(student_total) - jnp.log(teacher_total)

    def second_pass(grad_sum, pairs):
        teacher_logit, student_tanh = logits(pairs[0], pairs[1])
        teacher_prob = jnp.exp(teacher_logit) / teacher_total[:, None]
        student_prob = jnp.exp(softcap * student_tanh) / student_total[:, None]
        logit_grad = (kl_weight[:, None] * (student_prob - teacher_prob) * (1.0 - student_tanh * student_tanh)).astype(jnp.bfloat16)
        head_grad = jnp.dot(logit_grad.T, student_normed, preferred_element_type=jnp.float32).astype(jnp.bfloat16)
        grad_sum = grad_sum + jnp.dot(logit_grad, pairs[1], preferred_element_type=jnp.float32)
        return (grad_sum, head_grad)
    grad_normed, head_grads = lax.scan(second_pass, jnp.zeros((TOKENS, DS), jnp.float32), (teacher_blocks, student_blocks))
    grad_head = head_grads.reshape(VOCAB, DS)
    inner = lax.optimization_barrier(jnp.sum(raw_student * student_gain * grad_normed, axis=1, keepdims=True))
    cubed = student_scale * student_scale * student_scale
    grad_hidden = (student_scale * student_gain * grad_normed - raw_student * cubed * inner / DS).astype(jnp.bfloat16)
    return (token_kl, grad_hidden, grad_head)
```

```python
import jax
import jax.numpy as jnp
from jax import lax
from jax.sharding import Mesh
from jax.sharding import PartitionSpec as P

epsilon = 1e-06
softcap = 30.0
ROW = ("x", "yl")
VOC = ("yh", "z")
XY = ("x", "yl", "yh")
PLANE = ("x", "yl", "yh", "z")
bf16 = jnp.bfloat16
f32 = jnp.float32


def swap(value):
    return lax.ppermute(value, "c", [(0, 1), (1, 0)])


def spread(value, axes):
    count = lax.axis_size(axes)
    return lax.all_to_all(jnp.broadcast_to(value[None], (count, *value.shape)), axes, 0, 0)


def halves(value):
    high = lax.reduce_precision(value, 8, 7)
    return high.astype(bf16), (value - high).astype(bf16)


def dot_t(left, right):
    return lax.dot_general(left, right, (((1,), (1,)), ((), ())), preferred_element_type=f32)


def dot_0(left, right):
    return lax.dot_general(left, right, (((0,), (0,)), ((), ())), preferred_element_type=f32)


def local(
    context,
    residual_in,
    out_proj,
    post_gain,
    final_gain,
    teacher_head,
    student_hidden,
    student_gain,
    student_head,
    kl_weight,
):
    voc_count = lax.axis_size(VOC)
    row_count = lax.axis_size(ROW)
    rows = context.shape[0]
    teacher_cols = residual_in.shape[1]
    student_cols = student_hidden.shape[1]
    teacher_width = teacher_cols * voc_count
    student_width = student_cols * voc_count
    own = rows // voc_count
    half = rows * row_count
    voc_index = lax.axis_index(VOC)
    row_index = lax.axis_index(ROW)
    half_start = lax.axis_index("c") * half

    teacher_other = swap(teacher_head)
    student_other = swap(student_head)

    partial = jnp.dot(context, out_proj, preferred_element_type=f32).astype(bf16)
    raw_student = student_hidden.astype(f32)
    gains = jnp.stack(halves(jnp.concatenate([post_gain, final_gain])))
    squares = jnp.stack(halves(jnp.sum(raw_student * raw_student, axis=1)))
    shared = jnp.concatenate([gains, squares], axis=1)
    sent = jnp.concatenate(
        [
            partial.reshape(voc_count, own, teacher_width),
            residual_in.reshape(voc_count, own, teacher_cols),
            student_hidden.reshape(voc_count, own, student_cols),
            jnp.broadcast_to(shared[None], (voc_count, *shared.shape)),
        ],
        axis=2,
    )
    got = lax.all_to_all(sent, VOC, 0, 0)
    ends = [teacher_width, teacher_cols, student_cols, 2 * teacher_cols]
    at = [sum(ends[:i]) for i in range(5)]
    attention = jnp.sum(got[:, :, : at[1]].astype(f32), axis=0)
    residual = got[:, :, at[1] : at[2]].transpose(1, 0, 2).reshape(own, teacher_width)
    student_rows = got[:, :, at[2] : at[3]].transpose(1, 0, 2).reshape(own, student_width)
    gain_all = jnp.sum(got[:, :, at[3] : at[4]].astype(f32), axis=1)
    post_all = gain_all[:, :teacher_cols].reshape(teacher_width)
    final_all = gain_all[:, teacher_cols:].reshape(teacher_width)
    own_square = jnp.sum(got[:, :, at[4] :].astype(f32), axis=(0, 1))
    own_scale = lax.rsqrt(own_square / student_width + epsilon)

    post_scale = lax.rsqrt(jnp.mean(attention * attention, axis=1, keepdims=True) + epsilon)
    hidden = residual.astype(f32) + attention * post_scale * post_all
    final_scale = lax.rsqrt(jnp.mean(hidden * hidden, axis=1, keepdims=True) + epsilon)
    teacher_rows = (hidden * final_scale * final_all).astype(bf16)
    student_f = student_rows.astype(f32)
    row_scale = lax.rsqrt(jnp.mean(student_f * student_f, axis=1, keepdims=True) + epsilon)
    normed_rows = (student_f * row_scale * student_gain).astype(bf16)

    both = jnp.concatenate([teacher_rows, normed_rows], axis=1)
    both = spread(both, "z").reshape(-1, both.shape[1])
    both = spread(both, XY).reshape(half, -1)
    teacher_all = both[:, :teacher_width]
    student_all = both[:, teacher_width:]
    student_all_other = swap(student_all)

    def logits(teacher_rows_of, student_rows_of):
        teacher_logit = softcap * jnp.tanh(dot_t(teacher_all, teacher_rows_of) / softcap)
        student_tanh = jnp.tanh(dot_t(student_all, student_rows_of) / softcap)
        student_logit = softcap * student_tanh
        teacher_exp = jnp.exp(teacher_logit)
        student_exp = jnp.exp(student_logit)
        sums = jnp.stack(
            [
                jnp.sum(teacher_exp, axis=1),
                jnp.sum(student_exp, axis=1),
                jnp.sum(teacher_exp * (teacher_logit - student_logit), axis=1),
            ]
        )
        return teacher_exp, student_exp, student_tanh, sums

    mine = logits(teacher_head, student_head)
    others = logits(teacher_other, student_other)
    sums = (mine[3] + others[3]).reshape(-1, 128)
    totals = jnp.sum(spread(sums, PLANE), axis=0).reshape(3, half)
    teacher_total, student_total, mixed = totals[0], totals[1], totals[2]
    token_kl = mixed / teacher_total + jnp.log(student_total) - jnp.log(teacher_total)
    token_kl = lax.dynamic_slice_in_dim(token_kl, row_index * rows + voc_index * own, own)
    weight = lax.dynamic_slice_in_dim(kl_weight, half_start, half)

    def gradient(parts):
        teacher_prob = parts[0] / teacher_total[:, None]
        student_prob = parts[1] / student_total[:, None]
        return (
            weight[:, None] * (student_prob - teacher_prob) * (1.0 - parts[2] * parts[2])
        ).astype(bf16)

    grad_mine = gradient(mine)
    grad_others = gradient(others)
    grad_back = swap(grad_others)
    terms = (
        jnp.dot(grad_mine, student_head, preferred_element_type=f32)
        + jnp.dot(grad_others, student_other, preferred_element_type=f32)
    ).astype(bf16)
    parts = lax.all_to_all(terms.reshape(row_count, rows, student_width), ROW, 0, 0)
    grad_head = (dot_0(grad_mine, student_all) + dot_0(grad_back, student_all_other)).astype(bf16)
    grad_rows = jnp.sum(parts.astype(f32), axis=0)
    own_normed = lax.dynamic_slice_in_dim(student_all, row_index * rows, rows).astype(f32)
    inner = jnp.stack(halves(jnp.sum(own_normed * grad_rows, axis=1)), axis=1)
    last = jnp.concatenate(
        [
            grad_rows.astype(bf16).reshape(rows, voc_count, student_cols).transpose(1, 0, 2),
            jnp.broadcast_to(inner[None], (voc_count, *inner.shape)),
        ],
        axis=2,
    )
    last = jnp.sum(lax.all_to_all(last, VOC, 0, 0).astype(f32), axis=0)
    grad_normed = last[:, :student_cols]
    inner_total = jnp.sum(last[:, student_cols:], axis=1) / own_scale
    gain_piece = lax.dynamic_slice_in_dim(student_gain, voc_index * student_cols, student_cols)
    cubed = own_scale * own_scale * own_scale
    grad_hidden = (
        own_scale[:, None] * gain_piece * grad_normed
        - raw_student * cubed[:, None] * inner_total[:, None] / student_width
    ).astype(bf16)
    return (token_kl, grad_hidden, grad_head)


def solution(mesh):
    sec, tok, voc = mesh.devices.shape
    fine = Mesh(mesh.devices.reshape(sec, tok // 2, 2, 2, voc // 2), ("c", "x", "yl", "yh", "z"))
    row = ("c", "x", "yl")
    every = ("c", "x", "yl", "yh", "z")
    return jax.shard_map(
        local,
        mesh=fine,
        in_specs=(
            P(row, VOC),
            P(row, VOC),
            P(VOC, None),
            P(VOC),
            P(VOC),
            P(every, None),
            P(row, VOC),
            P(),
            P(every, None),
            P(),
        ),
        out_specs=(P(every), P(row, VOC), P(every, None)),
        check_vma=False,
    )
```

```python
import functools

import jax
import jax.numpy as jnp
from jax import lax
from jax.experimental import pallas as pl
from jax.experimental.pallas import tpu as pltpu
from jax.sharding import Mesh
from jax.sharding import PartitionSpec as P

epsilon = 1e-06
softcap = 30.0
ROW = ("x", "yl")
VOC = ("yh", "z")
XY = ("x", "yl", "yh")
bf16 = jnp.bfloat16
f32 = jnp.float32


def swap(value):
    return lax.ppermute(value, "c", [(0, 1), (1, 0)])


def spread(value, axes):
    count = lax.axis_size(axes)
    return lax.all_to_all(jnp.broadcast_to(value[None], (count, *value.shape)), axes, 0, 0)


def ring_step(right, left):
    count = lax.axis_size("z")
    return (
        lax.ppermute(right, "z", [(i, (i + 1) % count) for i in range(count)]),
        lax.ppermute(left, "z", [(i, (i - 1) % count) for i in range(count)]),
    )


def halves(value):
    high = lax.reduce_precision(value, 8, 7)
    return high.astype(bf16), (value - high).astype(bf16)


def dot_t(left, right):
    return lax.dot_general(left, right, (((1,), (1,)), ((), ())), preferred_element_type=f32)


def rows_kernel(cols, got, out):
    count, own, _ = got.shape
    width = out.shape[2]
    attention = jnp.zeros((own, width), f32)
    residual, post, final = [], [], []
    for i in range(count):
        attention += got[i, :, :width].astype(f32)
        rest = got[i, :, width:].astype(f32)
        residual.append(rest[:, :cols])
        gains = jnp.sum(rest[:, cols : 3 * cols], axis=0, keepdims=True)
        post.append(gains[:, :cols])
        final.append(gains[:, cols:])
    post_scale = lax.rsqrt(jnp.mean(attention * attention, axis=1, keepdims=True) + epsilon)
    hidden = jnp.concatenate(residual, axis=1) + attention * post_scale * jnp.concatenate(post, axis=1)
    final_scale = lax.rsqrt(jnp.mean(hidden * hidden, axis=1, keepdims=True) + epsilon)
    normed = (hidden * final_scale * jnp.concatenate(final, axis=1)).astype(bf16)
    for i in range(count):
        out[i] = normed


def own_rows(got, width, cols):
    vmem = pl.BlockSpec(memory_space=pltpu.VMEM)
    count, own, _ = got.shape
    return pl.pallas_call(
        functools.partial(rows_kernel, cols),
        out_shape=jax.ShapeDtypeStruct((count, own, width), bf16),
        in_specs=[vmem],
        out_specs=vmem,
        compiler_params=pltpu.CompilerParams(vmem_limit_bytes=56 * 2**20),
        cost_estimate=pl.CostEstimate(flops=got.size, bytes_accessed=4 * got.size, transcendentals=0),
    )(got)


def student_kernel(own_rows_count, gain, *refs):
    blocks = refs[:9]
    (own_head, other_head, normed_out, scale, own_tanh, other_tanh, sums) = refs[9:16]
    pieces, normed, held, tanhs, block_sem, sem = refs[16:]
    z_count, piece_rows, cols = pieces.shape
    z_index = lax.axis_index("z")
    copies = []
    for k, offset in enumerate((0, -1, 1, -2, 2, -3, 3, 4, 4)):
        place = pieces.at[lax.rem(z_index + (offset + z_count), z_count)]
        if k >= 7:
            place = place.at[pl.ds((k - 7) * (piece_rows // 2), piece_rows // 2)]
        copies.append(pltpu.make_async_copy(blocks[k], place, block_sem.at[k]))
        copies[k].start()
    chunk = held.shape[1]
    each = own_head.shape[0] // chunk
    heads = []
    for i in range(2 * each):
        head = own_head if i < each else other_head
        heads.append(
            pltpu.make_async_copy(head.at[pl.ds((i % each) * chunk, chunk)], held.at[i], sem.at[0, i])
        )
    for copy in copies:
        copy.wait()
    for copy in heads:
        copy.start()
    tokens, width = normed.shape
    highs = width // (z_count * cols)
    rows = own_rows_count
    for r in range(tokens // rows):
        raw = jnp.concatenate(
            [
                pieces[z, (r * highs + h) * rows : (r * highs + h + 1) * rows, :].astype(f32)
                for h in range(highs)
                for z in range(z_count)
            ],
            axis=1,
        )
        part_scale = lax.rsqrt(jnp.mean(raw * raw, axis=1, keepdims=True) + epsilon)
        part = pl.ds(r * rows, rows)
        scale[part, :] = part_scale
        normed[part, :] = (raw * part_scale * gain[...]).astype(bf16)
    stores = [pltpu.make_async_copy(normed, normed_out, sem.at[1, 2 * each])]
    stores[0].start()
    total = jnp.zeros((1, tokens), f32)
    for i in range(2 * each):
        part = pl.ds((i % each) * chunk, chunk)
        heads[i].wait()
        student = jnp.tanh(dot_t(held[i], normed[...]) * (1.0 / softcap))
        tanhs[i] = student
        out = own_tanh if i < each else other_tanh
        stores.append(pltpu.make_async_copy(tanhs.at[i], out.at[part], sem.at[1, i]))
        stores[-1].start()
        total += jnp.sum(jnp.exp(softcap * student), axis=0, keepdims=True)
    sums[...] = total
    for store in stores:
        store.wait()


def student_logits(rows, gain, blocks, own_head, other_head):
    count, width = own_head.shape
    piece_rows, cols = blocks[0].shape
    z_count = lax.axis_size("z")
    tokens = piece_rows * cols * z_count // width
    chunk = count // 2
    vmem = pl.BlockSpec(memory_space=pltpu.VMEM)
    anywhere = pl.BlockSpec(memory_space=pl.ANY)
    return pl.pallas_call(
        functools.partial(student_kernel, rows),
        out_shape=(
            jax.ShapeDtypeStruct((tokens, width), bf16),
            jax.ShapeDtypeStruct((tokens, 1), f32),
            jax.ShapeDtypeStruct((count, tokens), f32),
            jax.ShapeDtypeStruct((count, tokens), f32),
            jax.ShapeDtypeStruct((1, tokens), f32),
        ),
        in_specs=[vmem] + [anywhere] * 11,
        out_specs=(anywhere, vmem, anywhere, anywhere, vmem),
        scratch_shapes=[
            pltpu.VMEM((z_count, piece_rows, cols), bf16),
            pltpu.VMEM((tokens, width), bf16),
            pltpu.VMEM((4, chunk, width), bf16),
            pltpu.VMEM((4, chunk, tokens), f32),
            pltpu.SemaphoreType.DMA((9,)),
            pltpu.SemaphoreType.DMA((2, 5)),
        ],
        compiler_params=pltpu.CompilerParams(vmem_limit_bytes=56 * 2**20),
        cost_estimate=pl.CostEstimate(
            flops=4 * count * tokens * width,
            bytes_accessed=4 * count * width,
            transcendentals=4 * count * tokens,
        ),
    )(gain, *blocks, own_head, other_head)


def teacher_kernel(rows, own_head, other_head, own_tanh, other_tanh, own_exp, other_exp, sums):
    total = jnp.zeros((1, rows.shape[0]), f32)
    mixed = jnp.zeros((1, rows.shape[0]), f32)
    for head, tanh, out in ((own_head, own_tanh, own_exp), (other_head, other_tanh, other_exp)):
        logit = softcap * jnp.tanh(dot_t(rows[...], head[...]).T * (1.0 / softcap))
        grown = jnp.exp(logit)
        out[...] = grown
        total += jnp.sum(grown, axis=0, keepdims=True)
        mixed += jnp.sum(grown * (logit - softcap * tanh[...]), axis=0, keepdims=True)
    sums[...] = jnp.concatenate([total, mixed], axis=0)


def teacher_logits(rows, own_head, other_head, own_tanh, other_tanh):
    count, width = own_head.shape
    tokens = rows.shape[0]
    vmem = pl.BlockSpec(memory_space=pltpu.VMEM)
    return pl.pallas_call(
        teacher_kernel,
        out_shape=(
            jax.ShapeDtypeStruct((count, tokens), f32),
            jax.ShapeDtypeStruct((count, tokens), f32),
            jax.ShapeDtypeStruct((2, tokens), f32),
        ),
        in_specs=[vmem] * 5,
        out_specs=(vmem, vmem, vmem),
        compiler_params=pltpu.CompilerParams(vmem_limit_bytes=12 * 2**20),
        cost_estimate=pl.CostEstimate(
            flops=4 * count * tokens * width,
            bytes_accessed=4 * count * width,
            transcendentals=4 * count * tokens,
        ),
    )(rows, own_head, other_head, own_tanh, other_tanh)


def gradient_kernel(
    own_exp, other_exp, own_tanh, other_tanh, scales, own_head, other_head,
    own_grad, other_grad, terms, held, turned, sem,
):
    count = own_exp.shape[0]
    chunks, _, block = held.shape
    copies = []
    for i in range(chunks):
        columns = pl.ds(i * block, block)
        for j, head in enumerate((own_head, other_head)):
            copies.append(
                pltpu.make_async_copy(
                    head.at[:, columns], held.at[i, pl.ds(j * count, count)], sem.at[i, j]
                )
            )
            copies[-1].start()
    for start, exps, tanhs, grads in (
        (0, own_exp, own_tanh, own_grad),
        (count, other_exp, other_tanh, other_grad),
    ):
        student = tanhs[...]
        grad = (jnp.exp(softcap * student) * scales[0:1, :] - exps[...] * scales[1:2, :]) * (
            1.0 - student * student
        )
        grads[...] = grad.astype(bf16)
        turned[:, pl.ds(start, count)] = grad.T.astype(bf16)
    for i in range(chunks):
        copies[2 * i].wait()
        copies[2 * i + 1].wait()
        terms[:, pl.ds(i * block, block)] = jnp.dot(
            turned[...], held[i], preferred_element_type=f32
        ).astype(bf16)


def gradient_terms(own_exp, other_exp, own_tanh, other_tanh, scales, own_head, other_head):
    count, tokens = own_exp.shape
    width = own_head.shape[1]
    block = 512
    vmem = pl.BlockSpec(memory_space=pltpu.VMEM)
    anywhere = pl.BlockSpec(memory_space=pl.ANY)
    return pl.pallas_call(
        gradient_kernel,
        out_shape=(
            jax.ShapeDtypeStruct((count, tokens), bf16),
            jax.ShapeDtypeStruct((count, tokens), bf16),
            jax.ShapeDtypeStruct((tokens, width), bf16),
        ),
        in_specs=[vmem] * 5 + [anywhere] * 2,
        out_specs=(vmem, vmem, vmem),
        scratch_shapes=[
            pltpu.VMEM((width // block, 2 * count, block), bf16),
            pltpu.VMEM((tokens, 2 * count), bf16),
            pltpu.SemaphoreType.DMA((width // block, 2)),
        ],
        compiler_params=pltpu.CompilerParams(vmem_limit_bytes=56 * 2**20),
        cost_estimate=pl.CostEstimate(
            flops=4 * count * tokens * width,
            bytes_accessed=4 * count * width + 20 * count * tokens,
            transcendentals=2 * count * tokens,
        ),
    )(own_exp, other_exp, own_tanh, other_tanh, scales, own_head, other_head)


def reduced_kernel(parts, normed, out):
    total = parts[0].astype(f32)
    for i in range(1, parts.shape[0]):
        total += parts[i].astype(f32)
    inner = jnp.sum(normed[...].astype(f32) * total, axis=1, keepdims=True)
    high = inner.astype(bf16).astype(f32)
    count, rows, width = out.shape
    cols = total.shape[1] // count
    lane = lax.broadcasted_iota(jnp.int32, (rows, width - cols), 1)
    behind = jnp.where(lane == 0, high, jnp.where(lane == 1, inner - high, 0.0))
    for i in range(count):
        piece = jnp.concatenate([total[:, i * cols : (i + 1) * cols], behind], axis=1)
        out[i] = piece.astype(bf16)


def reduced_pieces(parts, normed, count, width):
    rows = normed.shape[0]
    vmem = pl.BlockSpec(memory_space=pltpu.VMEM)
    return pl.pallas_call(
        reduced_kernel,
        out_shape=jax.ShapeDtypeStruct((count, rows, width), bf16),
        in_specs=[vmem, vmem],
        out_specs=vmem,
        compiler_params=pltpu.CompilerParams(vmem_limit_bytes=56 * 2**20),
        cost_estimate=pl.CostEstimate(
            flops=parts.size, bytes_accessed=2 * parts.size, transcendentals=0
        ),
    )(parts, normed)


def local(
    context,
    residual_in,
    out_proj,
    post_gain,
    final_gain,
    teacher_head,
    student_hidden,
    student_gain,
    student_head,
    kl_weight,
):
    voc_count = lax.axis_size(VOC)
    row_count = lax.axis_size(ROW)
    rows = context.shape[0]
    teacher_cols = residual_in.shape[1]
    student_cols = student_hidden.shape[1]
    teacher_width = teacher_cols * voc_count
    student_width = student_cols * voc_count
    own = rows // voc_count
    half = rows * row_count
    voc_index = lax.axis_index(VOC)
    row_index = lax.axis_index(ROW)
    half_start = lax.axis_index("c") * half

    teacher_other = swap(teacher_head)
    student_other = swap(student_head)

    pieces = spread(student_hidden, XY).reshape(-1, student_cols)

    partial = jnp.dot(context, out_proj, preferred_element_type=f32).astype(bf16)
    raw_student = student_hidden.astype(f32)
    gains = jnp.stack(halves(jnp.concatenate([post_gain, final_gain])))
    sent = jnp.concatenate(
        [
            partial.reshape(voc_count, own, teacher_width),
            residual_in.reshape(voc_count, own, teacher_cols),
            jnp.broadcast_to(gains[None], (voc_count, *gains.shape)),
        ],
        axis=2,
    )
    got = lax.all_to_all(sent, VOC, 0, 0)
    teacher_rows = own_rows(got, teacher_width, teacher_cols)
    teacher_rows, pieces = lax.optimization_barrier((teacher_rows, pieces))
    right, left = ring_step(pieces, pieces)
    ring = [pieces, right, left]
    teacher_rows = lax.all_to_all(teacher_rows, VOC, 0, 0).reshape(rows, teacher_width)
    teacher_rows, right, left = lax.optimization_barrier((teacher_rows, right, left))
    right, left = ring_step(right, left)
    ring += [right, left]
    right, left = ring_step(right, left)
    ring += [right, left]
    cut = pieces.shape[0] // 2
    right, left = ring_step(right[:cut], left[cut:])
    ring += [right, left]
    teacher_all = spread(teacher_rows, ROW).reshape(half, teacher_width)

    student_all, student_scale, tanh_mine, tanh_others, student_sum = student_logits(
        rows, student_gain[None], ring, student_head, student_other
    )
    own_scale = lax.dynamic_slice_in_dim(student_scale[:, 0], row_index * rows, rows)
    exp_mine, exp_others, teacher_sums = teacher_logits(
        teacher_all, teacher_head, teacher_other, tanh_mine, tanh_others
    )
    sums = jnp.concatenate([teacher_sums, student_sum]).reshape(-1, 128)
    sums = jnp.sum(spread(sums, XY), axis=0)
    sums, student_tied = lax.optimization_barrier((sums, student_all))
    student_all_other = swap(student_tied)
    totals = jnp.sum(spread(sums, "z"), axis=0).reshape(3, half)
    teacher_total, mixed, student_total = totals[0], totals[1], totals[2]
    token_kl = mixed / teacher_total + jnp.log(student_total) - jnp.log(teacher_total)
    token_kl = lax.dynamic_slice_in_dim(token_kl, row_index * rows + voc_index * own, own)
    weight = lax.dynamic_slice_in_dim(kl_weight, half_start, half)
    scales = jnp.stack([weight / student_total, weight / teacher_total])

    grad_mine, grad_others, terms = gradient_terms(
        exp_mine, exp_others, tanh_mine, tanh_others, scales, student_head, student_other
    )
    grad_back = swap(grad_others)
    parts = lax.all_to_all(terms.reshape(row_count, rows, student_width), ROW, 0, 0)
    grad_head = (
        jnp.dot(grad_mine, student_all, preferred_element_type=f32)
        + jnp.dot(grad_back, student_all_other, preferred_element_type=f32)
    ).astype(bf16)
    own_normed = lax.dynamic_slice_in_dim(student_all, row_index * rows, rows)
    last = reduced_pieces(parts, own_normed, voc_count, 256)
    last = jnp.sum(lax.all_to_all(last, VOC, 0, 0).astype(f32), axis=0)
    grad_normed = last[:, :student_cols]
    inner_total = (last[:, student_cols] + last[:, student_cols + 1]) / own_scale
    gain_piece = lax.dynamic_slice_in_dim(student_gain, voc_index * student_cols, student_cols)
    cubed = own_scale * own_scale * own_scale
    grad_hidden = (
        own_scale[:, None] * gain_piece * grad_normed
        - raw_student * cubed[:, None] * inner_total[:, None] / student_width
    ).astype(bf16)
    return (token_kl, grad_hidden, grad_head)


def solution(mesh):
    sec, tok, voc = mesh.devices.shape
    fine = Mesh(mesh.devices.reshape(sec, tok // 2, 2, 2, voc // 2), ("c", "x", "yl", "yh", "z"))
    row = ("c", "x", "yl")
    every = ("c", "x", "yl", "yh", "z")
    return jax.shard_map(
        local,
        mesh=fine,
        in_specs=(
            P(row, VOC),
            P(row, VOC),
            P(VOC, None),
            P(VOC),
            P(VOC),
            P(every, None),
            P(row, VOC),
            P(),
            P(every, None),
            P(),
        ),
        out_specs=(P(every), P(row, VOC), P(every, None)),
        check_vma=False,
    )
```

```python
import functools

import jax
import jax.numpy as jnp
from jax import lax
from jax.experimental import pallas as pl
from jax.experimental.pallas import tpu as pltpu
from jax.sharding import Mesh
from jax.sharding import PartitionSpec as P

epsilon = 1e-06
softcap = 30.0
ROW = ("x", "yl")
VOC = ("yh", "z")
XY = ("x", "yl", "yh")
bf16 = jnp.bfloat16
f32 = jnp.float32


def swap(value):
    return lax.ppermute(value, "c", [(0, 1), (1, 0)])


def spread(value, axes):
    count = lax.axis_size(axes)
    return lax.all_to_all(jnp.broadcast_to(value[None], (count, *value.shape)), axes, 0, 0)


def ring_step(right, left):
    count = lax.axis_size("z")
    return (
        lax.ppermute(right, "z", [(i, (i + 1) % count) for i in range(count)]),
        lax.ppermute(left, "z", [(i, (i - 1) % count) for i in range(count)]),
    )


def halves(value):
    high = lax.reduce_precision(value, 8, 7)
    return high.astype(bf16), (value - high).astype(bf16)


def dot_t(left, right):
    return lax.dot_general(left, right, (((1,), (1,)), ((), ())), preferred_element_type=f32)


def rows_kernel(cols, got, out):
    count, own, _ = got.shape
    width = out.shape[2]
    attention = jnp.zeros((own, width), f32)
    residual, post, final = [], [], []
    for i in range(count):
        attention += got[i, :, :width].astype(f32)
        rest = got[i, :, width:].astype(f32)
        residual.append(rest[:, :cols])
        gains = jnp.sum(rest[:, cols : 3 * cols], axis=0, keepdims=True)
        post.append(gains[:, :cols])
        final.append(gains[:, cols:])
    post_scale = lax.rsqrt(jnp.mean(attention * attention, axis=1, keepdims=True) + epsilon)
    hidden = jnp.concatenate(residual, axis=1) + attention * post_scale * jnp.concatenate(post, axis=1)
    final_scale = lax.rsqrt(jnp.mean(hidden * hidden, axis=1, keepdims=True) + epsilon)
    normed = (hidden * final_scale * jnp.concatenate(final, axis=1)).astype(bf16)
    for i in range(count):
        out[i] = normed


def own_rows(got, width, cols):
    vmem = pl.BlockSpec(memory_space=pltpu.VMEM)
    count, own, _ = got.shape
    return pl.pallas_call(
        functools.partial(rows_kernel, cols),
        out_shape=jax.ShapeDtypeStruct((count, own, width), bf16),
        in_specs=[vmem],
        out_specs=vmem,
        compiler_params=pltpu.CompilerParams(vmem_limit_bytes=56 * 2**20),
        cost_estimate=pl.CostEstimate(flops=got.size, bytes_accessed=4 * got.size, transcendentals=0),
    )(got)


def student_kernel(own_rows_count, gain, *refs):
    blocks = refs[:9]
    (own_head, other_head, normed_out, scale, own_tanh, other_tanh, sums) = refs[9:16]
    pieces, normed, held, tanhs, block_sem, sem = refs[16:]
    z_count, piece_rows, cols = pieces.shape
    z_index = lax.axis_index("z")
    copies = []
    for k, offset in enumerate((0, -1, 1, -2, 2, -3, 3, 4, 4)):
        place = pieces.at[lax.rem(z_index + (offset + z_count), z_count)]
        if k >= 7:
            place = place.at[pl.ds((k - 7) * (piece_rows // 2), piece_rows // 2)]
        copies.append(pltpu.make_async_copy(blocks[k], place, block_sem.at[k]))
        copies[k].start()
    chunk = held.shape[1]
    each = own_head.shape[0] // chunk
    heads = []
    for i in range(2 * each):
        head = own_head if i < each else other_head
        heads.append(
            pltpu.make_async_copy(head.at[pl.ds((i % each) * chunk, chunk)], held.at[i], sem.at[0, i])
        )
    for copy in copies:
        copy.wait()
    for copy in heads:
        copy.start()
    tokens, width = normed.shape
    highs = width // (z_count * cols)
    rows = own_rows_count
    for r in range(tokens // rows):
        raw = jnp.concatenate(
            [
                pieces[z, (r * highs + h) * rows : (r * highs + h + 1) * rows, :].astype(f32)
                for h in range(highs)
                for z in range(z_count)
            ],
            axis=1,
        )
        part_scale = lax.rsqrt(jnp.mean(raw * raw, axis=1, keepdims=True) + epsilon)
        part = pl.ds(r * rows, rows)
        scale[part, :] = part_scale
        normed[part, :] = (raw * part_scale * gain[...]).astype(bf16)
    stores = [pltpu.make_async_copy(normed, normed_out, sem.at[1, 2 * each])]
    stores[0].start()
    total = jnp.zeros((1, tokens), f32)
    for i in range(2 * each):
        part = pl.ds((i % each) * chunk, chunk)
        heads[i].wait()
        student = jnp.tanh(dot_t(held[i], normed[...]) * (1.0 / softcap))
        tanhs[i] = student
        out = own_tanh if i < each else other_tanh
        stores.append(pltpu.make_async_copy(tanhs.at[i], out.at[part], sem.at[1, i]))
        stores[-1].start()
        total += jnp.sum(jnp.exp(softcap * student), axis=0, keepdims=True)
    sums[...] = total
    for store in stores:
        store.wait()


def student_logits(rows, gain, blocks, own_head, other_head):
    count, width = own_head.shape
    piece_rows, cols = blocks[0].shape
    z_count = lax.axis_size("z")
    tokens = piece_rows * cols * z_count // width
    chunk = count // 2
    vmem = pl.BlockSpec(memory_space=pltpu.VMEM)
    anywhere = pl.BlockSpec(memory_space=pl.ANY)
    return pl.pallas_call(
        functools.partial(student_kernel, rows),
        out_shape=(
            jax.ShapeDtypeStruct((tokens, width), bf16),
            jax.ShapeDtypeStruct((tokens, 1), f32),
            jax.ShapeDtypeStruct((count, tokens), f32),
            jax.ShapeDtypeStruct((count, tokens), f32),
            jax.ShapeDtypeStruct((1, tokens), f32),
        ),
        in_specs=[vmem] + [anywhere] * 11,
        out_specs=(anywhere, vmem, anywhere, anywhere, vmem),
        scratch_shapes=[
            pltpu.VMEM((z_count, piece_rows, cols), bf16),
            pltpu.VMEM((tokens, width), bf16),
            pltpu.VMEM((4, chunk, width), bf16),
            pltpu.VMEM((4, chunk, tokens), f32),
            pltpu.SemaphoreType.DMA((9,)),
            pltpu.SemaphoreType.DMA((2, 5)),
        ],
        compiler_params=pltpu.CompilerParams(vmem_limit_bytes=56 * 2**20),
        cost_estimate=pl.CostEstimate(
            flops=4 * count * tokens * width,
            bytes_accessed=4 * count * width,
            transcendentals=4 * count * tokens,
        ),
    )(gain, *blocks, own_head, other_head)


def teacher_kernel(rows, own_head, other_head, own_tanh, other_tanh, own_exp, other_exp, sums):
    total = jnp.zeros((1, rows.shape[0]), f32)
    mixed = jnp.zeros((1, rows.shape[0]), f32)
    for head, tanh, out in ((own_head, own_tanh, own_exp), (other_head, other_tanh, other_exp)):
        logit = softcap * jnp.tanh(dot_t(rows[...], head[...]).T * (1.0 / softcap))
        grown = jnp.exp(logit)
        out[...] = grown
        total += jnp.sum(grown, axis=0, keepdims=True)
        mixed += jnp.sum(grown * (logit - softcap * tanh[...]), axis=0, keepdims=True)
    sums[...] = jnp.concatenate([total, mixed], axis=0)


def teacher_logits(rows, own_head, other_head, own_tanh, other_tanh):
    count, width = own_head.shape
    tokens = rows.shape[0]
    vmem = pl.BlockSpec(memory_space=pltpu.VMEM)
    return pl.pallas_call(
        teacher_kernel,
        out_shape=(
            jax.ShapeDtypeStruct((count, tokens), f32),
            jax.ShapeDtypeStruct((count, tokens), f32),
            jax.ShapeDtypeStruct((2, tokens), f32),
        ),
        in_specs=[vmem] * 5,
        out_specs=(vmem, vmem, vmem),
        compiler_params=pltpu.CompilerParams(vmem_limit_bytes=12 * 2**20),
        cost_estimate=pl.CostEstimate(
            flops=4 * count * tokens * width,
            bytes_accessed=4 * count * width,
            transcendentals=4 * count * tokens,
        ),
    )(rows, own_head, other_head, own_tanh, other_tanh)


def gradient_kernel(
    own_exp, other_exp, own_tanh, other_tanh, scales, own_head, other_head,
    own_grad, other_grad, terms, held, turned, sem,
):
    count = own_exp.shape[0]
    chunks, _, block = held.shape
    copies = []
    for i in range(chunks):
        columns = pl.ds(i * block, block)
        for j, head in enumerate((own_head, other_head)):
            copies.append(
                pltpu.make_async_copy(
                    head.at[:, columns], held.at[i, pl.ds(j * count, count)], sem.at[i, j]
                )
            )
            copies[-1].start()
    for start, exps, tanhs, grads in (
        (0, own_exp, own_tanh, own_grad),
        (count, other_exp, other_tanh, other_grad),
    ):
        student = tanhs[...]
        grad = (jnp.exp(softcap * student) * scales[0:1, :] - exps[...] * scales[1:2, :]) * (
            1.0 - student * student
        )
        grads[...] = grad.astype(bf16)
        turned[:, pl.ds(start, count)] = grad.T.astype(bf16)
    for i in range(chunks):
        copies[2 * i].wait()
        copies[2 * i + 1].wait()
        terms[:, pl.ds(i * block, block)] = jnp.dot(
            turned[...], held[i], preferred_element_type=f32
        ).astype(bf16)


def gradient_terms(own_exp, other_exp, own_tanh, other_tanh, scales, own_head, other_head):
    count, tokens = own_exp.shape
    width = own_head.shape[1]
    block = 512
    vmem = pl.BlockSpec(memory_space=pltpu.VMEM)
    anywhere = pl.BlockSpec(memory_space=pl.ANY)
    return pl.pallas_call(
        gradient_kernel,
        out_shape=(
            jax.ShapeDtypeStruct((count, tokens), bf16),
            jax.ShapeDtypeStruct((count, tokens), bf16),
            jax.ShapeDtypeStruct((tokens, width), bf16),
        ),
        in_specs=[vmem] * 5 + [anywhere] * 2,
        out_specs=(vmem, vmem, vmem),
        scratch_shapes=[
            pltpu.VMEM((width // block, 2 * count, block), bf16),
            pltpu.VMEM((tokens, 2 * count), bf16),
            pltpu.SemaphoreType.DMA((width // block, 2)),
        ],
        compiler_params=pltpu.CompilerParams(vmem_limit_bytes=56 * 2**20),
        cost_estimate=pl.CostEstimate(
            flops=4 * count * tokens * width,
            bytes_accessed=4 * count * width + 20 * count * tokens,
            transcendentals=2 * count * tokens,
        ),
    )(own_exp, other_exp, own_tanh, other_tanh, scales, own_head, other_head)


def reduced_kernel(parts, normed, out):
    total = parts[0].astype(f32)
    for i in range(1, parts.shape[0]):
        total += parts[i].astype(f32)
    inner = jnp.sum(normed[...].astype(f32) * total, axis=1, keepdims=True)
    high = inner.astype(bf16).astype(f32)
    count, rows, width = out.shape
    cols = total.shape[1] // count
    lane = lax.broadcasted_iota(jnp.int32, (rows, width - cols), 1)
    behind = jnp.where(lane == 0, high, jnp.where(lane == 1, inner - high, 0.0))
    for i in range(count):
        piece = jnp.concatenate([total[:, i * cols : (i + 1) * cols], behind], axis=1)
        out[i] = piece.astype(bf16)


def reduced_pieces(parts, normed, count, width):
    rows = normed.shape[0]
    vmem = pl.BlockSpec(memory_space=pltpu.VMEM)
    return pl.pallas_call(
        reduced_kernel,
        out_shape=jax.ShapeDtypeStruct((count, rows, width), bf16),
        in_specs=[vmem, vmem],
        out_specs=vmem,
        compiler_params=pltpu.CompilerParams(vmem_limit_bytes=56 * 2**20),
        cost_estimate=pl.CostEstimate(
            flops=parts.size, bytes_accessed=2 * parts.size, transcendentals=0
        ),
    )(parts, normed)


def local(
    context,
    residual_in,
    out_proj,
    post_gain,
    final_gain,
    teacher_head,
    student_hidden,
    student_gain,
    student_head,
    kl_weight,
):
    voc_count = lax.axis_size(VOC)
    row_count = lax.axis_size(ROW)
    rows = context.shape[0]
    teacher_cols = residual_in.shape[1]
    student_cols = student_hidden.shape[1]
    teacher_width = teacher_cols * voc_count
    student_width = student_cols * voc_count
    own = rows // voc_count
    half = rows * row_count
    voc_index = lax.axis_index(VOC)
    row_index = lax.axis_index(ROW)
    half_start = lax.axis_index("c") * half

    teacher_other = swap(teacher_head)
    student_other = swap(student_head)

    pieces = spread(student_hidden, XY).reshape(-1, student_cols)

    partial = jnp.dot(context, out_proj, preferred_element_type=f32).astype(bf16)
    raw_student = student_hidden.astype(f32)
    gains = jnp.stack(halves(jnp.concatenate([post_gain, final_gain])))
    sent = jnp.concatenate(
        [
            partial.reshape(voc_count, own, teacher_width),
            residual_in.reshape(voc_count, own, teacher_cols),
            jnp.broadcast_to(gains[None], (voc_count, *gains.shape)),
        ],
        axis=2,
    )
    right, left = ring_step(pieces, pieces)
    got = lax.all_to_all(sent, VOC, 0, 0)
    teacher_rows = own_rows(got, teacher_width, teacher_cols)
    ring = [pieces, right, left]
    teacher_rows, right, left = lax.optimization_barrier((teacher_rows, right, left))
    teacher_rows = lax.all_to_all(teacher_rows, VOC, 0, 0).reshape(rows, teacher_width)
    teacher_rows, right, left = lax.optimization_barrier((teacher_rows, right, left))
    right, left = ring_step(right, left)
    ring += [right, left]
    right, left = ring_step(right, left)
    ring += [right, left]
    cut = pieces.shape[0] // 2
    right, left = ring_step(right[:cut], left[cut:])
    ring += [right, left]
    teacher_all = spread(teacher_rows, ROW).reshape(half, teacher_width)

    student_all, student_scale, tanh_mine, tanh_others, student_sum = student_logits(
        rows, student_gain[None], ring, student_head, student_other
    )
    own_scale = lax.dynamic_slice_in_dim(student_scale[:, 0], row_index * rows, rows)
    exp_mine, exp_others, teacher_sums = teacher_logits(
        teacher_all, teacher_head, teacher_other, tanh_mine, tanh_others
    )
    sums = jnp.concatenate([teacher_sums, student_sum]).reshape(-1, 128)
    sums, student_tied = lax.optimization_barrier((sums, student_all))
    student_all_other = swap(student_tied)
    totals = jnp.sum(spread(sums, ("x", "yl", "yh", "z")), axis=0).reshape(3, half)
    teacher_total, mixed, student_total = totals[0], totals[1], totals[2]
    token_kl = mixed / teacher_total + jnp.log(student_total) - jnp.log(teacher_total)
    token_kl = lax.dynamic_slice_in_dim(token_kl, row_index * rows + voc_index * own, own)
    weight = lax.dynamic_slice_in_dim(kl_weight, half_start, half)
    scales = jnp.stack([weight / student_total, weight / teacher_total])

    grad_mine, grad_others, terms = gradient_terms(
        exp_mine, exp_others, tanh_mine, tanh_others, scales, student_head, student_other
    )
    grad_back = swap(grad_others)
    parts = lax.all_to_all(terms.reshape(row_count, rows, student_width), ROW, 0, 0)
    grad_head = (
        jnp.dot(grad_mine, student_all, preferred_element_type=f32)
        + jnp.dot(grad_back, student_all_other, preferred_element_type=f32)
    ).astype(bf16)
    own_normed = lax.dynamic_slice_in_dim(student_all, row_index * rows, rows)
    last = reduced_pieces(parts, own_normed, voc_count, 256)
    last = jnp.sum(lax.all_to_all(last, VOC, 0, 0).astype(f32), axis=0)
    grad_normed = last[:, :student_cols]
    inner_total = (last[:, student_cols] + last[:, student_cols + 1]) / own_scale
    gain_piece = lax.dynamic_slice_in_dim(student_gain, voc_index * student_cols, student_cols)
    cubed = own_scale * own_scale * own_scale
    grad_hidden = (
        own_scale[:, None] * gain_piece * grad_normed
        - raw_student * cubed[:, None] * inner_total[:, None] / student_width
    ).astype(bf16)
    return (token_kl, grad_hidden, grad_head)


def solution(mesh):
    sec, tok, voc = mesh.devices.shape
    fine = Mesh(mesh.devices.reshape(sec, tok // 2, 2, 2, voc // 2), ("c", "x", "yl", "yh", "z"))
    row = ("c", "x", "yl")
    every = ("c", "x", "yl", "yh", "z")
    return jax.shard_map(
        local,
        mesh=fine,
        in_specs=(
            P(row, VOC),
            P(row, VOC),
            P(VOC, None),
            P(VOC),
            P(VOC),
            P(every, None),
            P(row, VOC),
            P(),
            P(every, None),
            P(),
        ),
        out_specs=(P(every), P(row, VOC), P(every, None)),
        check_vma=False,
    )
```

```python
import functools

import jax
import jax.numpy as jnp
from jax import lax
from jax.experimental import pallas as pl
from jax.experimental.pallas import tpu as pltpu
from jax.sharding import Mesh
from jax.sharding import PartitionSpec as P

epsilon = 1e-06
softcap = 30.0
ROW = ("x", "yl")
VOC = ("yh", "z")
XY = ("x", "yl", "yh")
bf16 = jnp.bfloat16
f32 = jnp.float32


def swap(value):
    return lax.ppermute(value, "c", [(0, 1), (1, 0)])


def spread(value, axes):
    count = lax.axis_size(axes)
    return lax.all_to_all(jnp.broadcast_to(value[None], (count, *value.shape)), axes, 0, 0)


def ring_step(right, left):
    count = lax.axis_size("z")
    return (
        lax.ppermute(right, "z", [(i, (i + 1) % count) for i in range(count)]),
        lax.ppermute(left, "z", [(i, (i - 1) % count) for i in range(count)]),
    )


def halves(value):
    high = lax.reduce_precision(value, 8, 7)
    return high.astype(bf16), (value - high).astype(bf16)


def dot_t(left, right):
    return lax.dot_general(left, right, (((1,), (1,)), ((), ())), preferred_element_type=f32)


def rows_kernel(cols, got, out):
    count, own, _ = got.shape
    width = out.shape[2]
    attention = jnp.zeros((own, width), f32)
    residual, post, final = [], [], []
    for i in range(count):
        attention += got[i, :, :width].astype(f32)
        rest = got[i, :, width:].astype(f32)
        residual.append(rest[:, :cols])
        gains = jnp.sum(rest[:, cols : 3 * cols], axis=0, keepdims=True)
        post.append(gains[:, :cols])
        final.append(gains[:, cols:])
    post_scale = lax.rsqrt(jnp.mean(attention * attention, axis=1, keepdims=True) + epsilon)
    hidden = jnp.concatenate(residual, axis=1) + attention * post_scale * jnp.concatenate(post, axis=1)
    final_scale = lax.rsqrt(jnp.mean(hidden * hidden, axis=1, keepdims=True) + epsilon)
    normed = (hidden * final_scale * jnp.concatenate(final, axis=1)).astype(bf16)
    for i in range(count):
        out[i] = normed


def own_rows(got, width, cols):
    vmem = pl.BlockSpec(memory_space=pltpu.VMEM)
    count, own, _ = got.shape
    return pl.pallas_call(
        functools.partial(rows_kernel, cols),
        out_shape=jax.ShapeDtypeStruct((count, own, width), bf16),
        in_specs=[vmem],
        out_specs=vmem,
        compiler_params=pltpu.CompilerParams(vmem_limit_bytes=56 * 2**20),
        cost_estimate=pl.CostEstimate(flops=got.size, bytes_accessed=4 * got.size, transcendentals=0),
    )(got)


def student_kernel(own_rows_count, gain, *refs):
    blocks = refs[:9]
    (own_head, other_head, normed_out, scale, own_tanh, other_tanh, sums) = refs[9:16]
    pieces, normed, held, tanhs, block_sem, sem = refs[16:]
    z_count, piece_rows, cols = pieces.shape
    z_index = lax.axis_index("z")
    copies = []
    for k, offset in enumerate((0, -1, 1, -2, 2, -3, 3, 4, 4)):
        place = pieces.at[lax.rem(z_index + (offset + z_count), z_count)]
        if k >= 7:
            place = place.at[pl.ds((k - 7) * (piece_rows // 2), piece_rows // 2)]
        copies.append(pltpu.make_async_copy(blocks[k], place, block_sem.at[k]))
        copies[k].start()
    chunk = held.shape[1]
    each = own_head.shape[0] // chunk
    heads = []
    for i in range(2 * each):
        head = own_head if i < each else other_head
        heads.append(
            pltpu.make_async_copy(head.at[pl.ds((i % each) * chunk, chunk)], held.at[i], sem.at[0, i])
        )
    for copy in copies:
        copy.wait()
    for copy in heads:
        copy.start()
    tokens, width = normed.shape
    highs = width // (z_count * cols)
    rows = own_rows_count
    for r in range(tokens // rows):
        raw = jnp.concatenate(
            [
                pieces[z, (r * highs + h) * rows : (r * highs + h + 1) * rows, :].astype(f32)
                for h in range(highs)
                for z in range(z_count)
            ],
            axis=1,
        )
        part_scale = lax.rsqrt(jnp.mean(raw * raw, axis=1, keepdims=True) + epsilon)
        part = pl.ds(r * rows, rows)
        scale[part, :] = part_scale
        normed[part, :] = (raw * part_scale * gain[...]).astype(bf16)
    stores = [pltpu.make_async_copy(normed, normed_out, sem.at[1, 2 * each])]
    stores[0].start()
    total = jnp.zeros((1, tokens), f32)
    for i in range(2 * each):
        part = pl.ds((i % each) * chunk, chunk)
        heads[i].wait()
        student = jnp.tanh(dot_t(held[i], normed[...]) * (1.0 / softcap))
        tanhs[i] = student
        out = own_tanh if i < each else other_tanh
        stores.append(pltpu.make_async_copy(tanhs.at[i], out.at[part], sem.at[1, i]))
        stores[-1].start()
        total += jnp.sum(jnp.exp(softcap * student), axis=0, keepdims=True)
    sums[...] = total
    for store in stores:
        store.wait()


def student_logits(rows, gain, blocks, own_head, other_head):
    count, width = own_head.shape
    piece_rows, cols = blocks[0].shape
    z_count = lax.axis_size("z")
    tokens = piece_rows * cols * z_count // width
    chunk = count // 2
    vmem = pl.BlockSpec(memory_space=pltpu.VMEM)
    anywhere = pl.BlockSpec(memory_space=pl.ANY)
    return pl.pallas_call(
        functools.partial(student_kernel, rows),
        out_shape=(
            jax.ShapeDtypeStruct((tokens, width), bf16),
            jax.ShapeDtypeStruct((tokens, 1), f32),
            jax.ShapeDtypeStruct((count, tokens), f32),
            jax.ShapeDtypeStruct((count, tokens), f32),
            jax.ShapeDtypeStruct((1, tokens), f32),
        ),
        in_specs=[vmem] + [anywhere] * 11,
        out_specs=(anywhere, vmem, anywhere, anywhere, vmem),
        scratch_shapes=[
            pltpu.VMEM((z_count, piece_rows, cols), bf16),
            pltpu.VMEM((tokens, width), bf16),
            pltpu.VMEM((4, chunk, width), bf16),
            pltpu.VMEM((4, chunk, tokens), f32),
            pltpu.SemaphoreType.DMA((9,)),
            pltpu.SemaphoreType.DMA((2, 5)),
        ],
        compiler_params=pltpu.CompilerParams(vmem_limit_bytes=56 * 2**20),
        cost_estimate=pl.CostEstimate(
            flops=4 * count * tokens * width,
            bytes_accessed=4 * count * width,
            transcendentals=4 * count * tokens,
        ),
    )(gain, *blocks, own_head, other_head)


def teacher_kernel(
    rows, own_head, other_head, own_tanh, other_tanh, own_exp, other_exp, sums, tanhs, sem
):
    loads = [
        pltpu.make_async_copy(own_tanh, tanhs.at[0], sem.at[0]),
        pltpu.make_async_copy(other_tanh, tanhs.at[1], sem.at[1]),
    ]
    for load in loads:
        load.start()
    total = jnp.zeros((1, rows.shape[0]), f32)
    mixed = jnp.zeros((1, rows.shape[0]), f32)
    for i, (head, out) in enumerate(((own_head, own_exp), (other_head, other_exp))):
        logit = softcap * jnp.tanh(dot_t(rows[...], head[...]).T * (1.0 / softcap))
        grown = jnp.exp(logit)
        out[...] = grown
        loads[i].wait()
        total += jnp.sum(grown, axis=0, keepdims=True)
        mixed += jnp.sum(grown * (logit - softcap * tanhs[i]), axis=0, keepdims=True)
    sums[...] = jnp.concatenate([total, mixed], axis=0)


def teacher_logits(rows, own_head, other_head, own_tanh, other_tanh):
    count, width = own_head.shape
    tokens = rows.shape[0]
    vmem = pl.BlockSpec(memory_space=pltpu.VMEM)
    return pl.pallas_call(
        teacher_kernel,
        out_shape=(
            jax.ShapeDtypeStruct((count, tokens), f32),
            jax.ShapeDtypeStruct((count, tokens), f32),
            jax.ShapeDtypeStruct((2, tokens), f32),
        ),
        in_specs=[vmem] * 3 + [pl.BlockSpec(memory_space=pl.ANY)] * 2,
        out_specs=(vmem, vmem, vmem),
        scratch_shapes=[pltpu.VMEM((2, count, tokens), f32), pltpu.SemaphoreType.DMA((2,))],
        compiler_params=pltpu.CompilerParams(vmem_limit_bytes=12 * 2**20),
        cost_estimate=pl.CostEstimate(
            flops=4 * count * tokens * width,
            bytes_accessed=4 * count * width,
            transcendentals=4 * count * tokens,
        ),
    )(rows, own_head, other_head, own_tanh, other_tanh)


def gradient_kernel(
    own_exp, other_exp, own_tanh, other_tanh, scales, own_head, other_head,
    own_grad, other_grad, terms, held, turned, sem,
):
    count = own_exp.shape[0]
    chunks, _, block = held.shape
    copies = []
    for i in range(chunks):
        columns = pl.ds(i * block, block)
        for j, head in enumerate((own_head, other_head)):
            copies.append(
                pltpu.make_async_copy(
                    head.at[:, columns], held.at[i, pl.ds(j * count, count)], sem.at[i, j]
                )
            )
            copies[-1].start()
    for start, exps, tanhs, grads in (
        (0, own_exp, own_tanh, own_grad),
        (count, other_exp, other_tanh, other_grad),
    ):
        student = tanhs[...]
        grad = (jnp.exp(softcap * student) * scales[0:1, :] - exps[...] * scales[1:2, :]) * (
            1.0 - student * student
        )
        grads[...] = grad.astype(bf16)
        turned[:, pl.ds(start, count)] = grad.T.astype(bf16)
    for i in range(chunks):
        copies[2 * i].wait()
        copies[2 * i + 1].wait()
        terms[:, pl.ds(i * block, block)] = jnp.dot(
            turned[...], held[i], preferred_element_type=f32
        ).astype(bf16)


def gradient_terms(own_exp, other_exp, own_tanh, other_tanh, scales, own_head, other_head):
    count, tokens = own_exp.shape
    width = own_head.shape[1]
    block = 512
    vmem = pl.BlockSpec(memory_space=pltpu.VMEM)
    anywhere = pl.BlockSpec(memory_space=pl.ANY)
    return pl.pallas_call(
        gradient_kernel,
        out_shape=(
            jax.ShapeDtypeStruct((count, tokens), bf16),
            jax.ShapeDtypeStruct((count, tokens), bf16),
            jax.ShapeDtypeStruct((tokens, width), bf16),
        ),
        in_specs=[vmem] * 5 + [anywhere] * 2,
        out_specs=(vmem, vmem, vmem),
        scratch_shapes=[
            pltpu.VMEM((width // block, 2 * count, block), bf16),
            pltpu.VMEM((tokens, 2 * count), bf16),
            pltpu.SemaphoreType.DMA((width // block, 2)),
        ],
        compiler_params=pltpu.CompilerParams(vmem_limit_bytes=56 * 2**20),
        cost_estimate=pl.CostEstimate(
            flops=4 * count * tokens * width,
            bytes_accessed=4 * count * width + 20 * count * tokens,
            transcendentals=2 * count * tokens,
        ),
    )(own_exp, other_exp, own_tanh, other_tanh, scales, own_head, other_head)


def reduced_kernel(parts, normed, out):
    total = parts[0].astype(f32)
    for i in range(1, parts.shape[0]):
        total += parts[i].astype(f32)
    inner = jnp.sum(normed[...].astype(f32) * total, axis=1, keepdims=True)
    high = inner.astype(bf16).astype(f32)
    count, rows, width = out.shape
    cols = total.shape[1] // count
    lane = lax.broadcasted_iota(jnp.int32, (rows, width - cols), 1)
    behind = jnp.where(lane == 0, high, jnp.where(lane == 1, inner - high, 0.0))
    for i in range(count):
        piece = jnp.concatenate([total[:, i * cols : (i + 1) * cols], behind], axis=1)
        out[i] = piece.astype(bf16)


def reduced_pieces(parts, normed, count, width):
    rows = normed.shape[0]
    vmem = pl.BlockSpec(memory_space=pltpu.VMEM)
    return pl.pallas_call(
        reduced_kernel,
        out_shape=jax.ShapeDtypeStruct((count, rows, width), bf16),
        in_specs=[vmem, vmem],
        out_specs=vmem,
        compiler_params=pltpu.CompilerParams(vmem_limit_bytes=56 * 2**20),
        cost_estimate=pl.CostEstimate(
            flops=parts.size, bytes_accessed=2 * parts.size, transcendentals=0
        ),
    )(parts, normed)


def local(
    context,
    residual_in,
    out_proj,
    post_gain,
    final_gain,
    teacher_head,
    student_hidden,
    student_gain,
    student_head,
    kl_weight,
):
    voc_count = lax.axis_size(VOC)
    row_count = lax.axis_size(ROW)
    rows = context.shape[0]
    teacher_cols = residual_in.shape[1]
    student_cols = student_hidden.shape[1]
    teacher_width = teacher_cols * voc_count
    student_width = student_cols * voc_count
    own = rows // voc_count
    half = rows * row_count
    voc_index = lax.axis_index(VOC)
    row_index = lax.axis_index(ROW)
    half_start = lax.axis_index("c") * half

    teacher_other = swap(teacher_head)
    student_other = swap(student_head)

    pieces = spread(student_hidden, XY).reshape(-1, student_cols)

    partial = jnp.dot(context, out_proj, preferred_element_type=f32).astype(bf16)
    raw_student = student_hidden.astype(f32)
    gains = jnp.stack(halves(jnp.concatenate([post_gain, final_gain])))
    sent = jnp.concatenate(
        [
            partial.reshape(voc_count, own, teacher_width),
            residual_in.reshape(voc_count, own, teacher_cols),
            jnp.broadcast_to(gains[None], (voc_count, *gains.shape)),
        ],
        axis=2,
    )
    right, left = ring_step(pieces, pieces)
    got = lax.all_to_all(sent, VOC, 0, 0)
    teacher_rows = own_rows(got, teacher_width, teacher_cols)
    ring = [pieces, right, left]
    teacher_rows, right, left = lax.optimization_barrier((teacher_rows, right, left))
    teacher_rows = lax.all_to_all(teacher_rows, VOC, 0, 0).reshape(rows, teacher_width)
    teacher_rows, right, left = lax.optimization_barrier((teacher_rows, right, left))
    right, left = ring_step(right, left)
    ring += [right, left]
    right, left = ring_step(right, left)
    ring += [right, left]
    cut = pieces.shape[0] // 2
    right, left = ring_step(right[:cut], left[cut:])
    ring += [right, left]
    teacher_all = spread(teacher_rows, ROW).reshape(half, teacher_width)

    student_all, student_scale, tanh_mine, tanh_others, student_sum = student_logits(
        rows, student_gain[None], ring, student_head, student_other
    )
    own_scale = lax.dynamic_slice_in_dim(student_scale[:, 0], row_index * rows, rows)
    exp_mine, exp_others, teacher_sums = teacher_logits(
        teacher_all, teacher_head, teacher_other, tanh_mine, tanh_others
    )
    sums = jnp.concatenate([teacher_sums, student_sum]).reshape(-1, 128)
    sums, student_tied = lax.optimization_barrier((sums, student_all))
    student_all_other = swap(student_tied)
    totals = jnp.sum(spread(sums, ("x", "yl", "yh", "z")), axis=0).reshape(3, half)
    teacher_total, mixed, student_total = totals[0], totals[1], totals[2]
    token_kl = mixed / teacher_total + jnp.log(student_total) - jnp.log(teacher_total)
    token_kl = lax.dynamic_slice_in_dim(token_kl, row_index * rows + voc_index * own, own)
    weight = lax.dynamic_slice_in_dim(kl_weight, half_start, half)
    scales = jnp.stack([weight / student_total, weight / teacher_total])

    grad_mine, grad_others, terms = gradient_terms(
        exp_mine, exp_others, tanh_mine, tanh_others, scales, student_head, student_other
    )
    grad_back = swap(grad_others)
    parts = lax.all_to_all(terms.reshape(row_count, rows, student_width), ROW, 0, 0)
    grad_head = (
        jnp.dot(grad_mine, student_all, preferred_element_type=f32)
        + jnp.dot(grad_back, student_all_other, preferred_element_type=f32)
    ).astype(bf16)
    own_normed = lax.dynamic_slice_in_dim(student_all, row_index * rows, rows)
    last = reduced_pieces(parts, own_normed, voc_count, 256)
    last = jnp.sum(lax.all_to_all(last, VOC, 0, 0).astype(f32), axis=0)
    grad_normed = last[:, :student_cols]
    inner_total = (last[:, student_cols] + last[:, student_cols + 1]) / own_scale
    gain_piece = lax.dynamic_slice_in_dim(student_gain, voc_index * student_cols, student_cols)
    cubed = own_scale * own_scale * own_scale
    grad_hidden = (
        own_scale[:, None] * gain_piece * grad_normed
        - raw_student * cubed[:, None] * inner_total[:, None] / student_width
    ).astype(bf16)
    return (token_kl, grad_hidden, grad_head)


def solution(mesh):
    sec, tok, voc = mesh.devices.shape
    fine = Mesh(mesh.devices.reshape(sec, tok // 2, 2, 2, voc // 2), ("c", "x", "yl", "yh", "z"))
    row = ("c", "x", "yl")
    every = ("c", "x", "yl", "yh", "z")
    return jax.shard_map(
        local,
        mesh=fine,
        in_specs=(
            P(row, VOC),
            P(row, VOC),
            P(VOC, None),
            P(VOC),
            P(VOC),
            P(every, None),
            P(row, VOC),
            P(),
            P(every, None),
            P(),
        ),
        out_specs=(P(every), P(row, VOC), P(every, None)),
        check_vma=False,
    )
```

```python
import functools

import jax
import jax.numpy as jnp
from jax import lax
from jax.experimental import pallas as pl
from jax.experimental.pallas import tpu as pltpu
from jax.sharding import Mesh
from jax.sharding import PartitionSpec as P

epsilon = 1e-06
softcap = 30.0
ROW = ("x", "yl")
VOC = ("yh", "z")
XY = ("x", "yl", "yh")
PLANE = ("x", "yl", "yh", "z")
bf16 = jnp.bfloat16
f32 = jnp.float32


def swap(value):
    return lax.ppermute(value, "c", [(0, 1), (1, 0)])


def spread(value, axes):
    count = lax.axis_size(axes)
    return lax.all_to_all(jnp.broadcast_to(value[None], (count, *value.shape)), axes, 0, 0)


def ring_step(right, left):
    count = lax.axis_size("z")
    return (
        lax.ppermute(right, "z", [(i, (i + 1) % count) for i in range(count)]),
        lax.ppermute(left, "z", [(i, (i - 1) % count) for i in range(count)]),
    )


def halves(value):
    high = lax.reduce_precision(value, 8, 7)
    return high.astype(bf16), (value - high).astype(bf16)


def dot_t(left, right):
    return lax.dot_general(left, right, (((1,), (1,)), ((), ())), preferred_element_type=f32)


def rows_kernel(cols, got, out):
    count, own, _ = got.shape
    width = out.shape[2]
    attention = jnp.zeros((own, width), f32)
    residual, post, final = [], [], []
    for i in range(count):
        attention += got[i, :, :width].astype(f32)
        rest = got[i, :, width:].astype(f32)
        residual.append(rest[:, :cols])
        gains = jnp.sum(rest[:, cols : 3 * cols], axis=0, keepdims=True)
        post.append(gains[:, :cols])
        final.append(gains[:, cols:])
    post_scale = lax.rsqrt(jnp.mean(attention * attention, axis=1, keepdims=True) + epsilon)
    hidden = jnp.concatenate(residual, axis=1) + attention * post_scale * jnp.concatenate(post, axis=1)
    final_scale = lax.rsqrt(jnp.mean(hidden * hidden, axis=1, keepdims=True) + epsilon)
    normed = (hidden * final_scale * jnp.concatenate(final, axis=1)).astype(bf16)
    for i in range(count):
        out[i] = normed


def own_rows(got, width, cols):
    vmem = pl.BlockSpec(memory_space=pltpu.VMEM)
    count, own, _ = got.shape
    return pl.pallas_call(
        functools.partial(rows_kernel, cols),
        out_shape=jax.ShapeDtypeStruct((count, own, width), bf16),
        in_specs=[vmem],
        out_specs=vmem,
        compiler_params=pltpu.CompilerParams(vmem_limit_bytes=56 * 2**20),
        cost_estimate=pl.CostEstimate(flops=got.size, bytes_accessed=4 * got.size, transcendentals=0),
    )(got)


def student_kernel(own_rows_count, gain, *refs):
    blocks = refs[:9]
    (own_head, other_head, normed_out, scale, own_tanh, other_tanh, sums) = refs[9:16]
    pieces, normed, held, tanhs, block_sem, sem = refs[16:]
    z_count, piece_rows, cols = pieces.shape
    z_index = lax.axis_index("z")
    copies = []
    for k, offset in enumerate((0, -1, 1, -2, 2, -3, 3, 4, 4)):
        place = pieces.at[lax.rem(z_index + (offset + z_count), z_count)]
        if k >= 7:
            place = place.at[pl.ds((k - 7) * (piece_rows // 2), piece_rows // 2)]
        copies.append(pltpu.make_async_copy(blocks[k], place, block_sem.at[k]))
        copies[k].start()
    chunk = held.shape[1]
    each = own_head.shape[0] // chunk
    heads = []
    for i in range(2 * each):
        head = own_head if i < each else other_head
        heads.append(
            pltpu.make_async_copy(head.at[pl.ds((i % each) * chunk, chunk)], held.at[i], sem.at[0, i])
        )
    for copy in copies:
        copy.wait()
    for copy in heads:
        copy.start()
    tokens, width = normed.shape
    highs = width // (z_count * cols)
    rows = own_rows_count
    for r in range(tokens // rows):
        raw = jnp.concatenate(
            [
                pieces[z, (r * highs + h) * rows : (r * highs + h + 1) * rows, :].astype(f32)
                for h in range(highs)
                for z in range(z_count)
            ],
            axis=1,
        )
        part_scale = lax.rsqrt(jnp.mean(raw * raw, axis=1, keepdims=True) + epsilon)
        part = pl.ds(r * rows, rows)
        scale[part, :] = part_scale
        normed[part, :] = (raw * part_scale * gain[...]).astype(bf16)
    stores = [pltpu.make_async_copy(normed, normed_out, sem.at[1, 2 * each])]
    stores[0].start()
    total = jnp.zeros((1, tokens), f32)
    for i in range(2 * each):
        part = pl.ds((i % each) * chunk, chunk)
        heads[i].wait()
        student = jnp.tanh(dot_t(held[i], normed[...]) * (1.0 / softcap))
        tanhs[i] = student
        out = own_tanh if i < each else other_tanh
        stores.append(pltpu.make_async_copy(tanhs.at[i], out.at[part], sem.at[1, i]))
        stores[-1].start()
        total += jnp.sum(jnp.exp(softcap * student), axis=0, keepdims=True)
    sums[...] = total
    for store in stores:
        store.wait()


def student_logits(rows, gain, blocks, own_head, other_head):
    count, width = own_head.shape
    piece_rows, cols = blocks[0].shape
    z_count = lax.axis_size("z")
    tokens = piece_rows * cols * z_count // width
    chunk = count // 2
    vmem = pl.BlockSpec(memory_space=pltpu.VMEM)
    anywhere = pl.BlockSpec(memory_space=pl.ANY)
    return pl.pallas_call(
        functools.partial(student_kernel, rows),
        out_shape=(
            jax.ShapeDtypeStruct((tokens, width), bf16),
            jax.ShapeDtypeStruct((tokens, 1), f32),
            jax.ShapeDtypeStruct((count, tokens), f32),
            jax.ShapeDtypeStruct((count, tokens), f32),
            jax.ShapeDtypeStruct((1, tokens), f32),
        ),
        in_specs=[vmem] + [anywhere] * 11,
        out_specs=(anywhere, vmem, anywhere, anywhere, vmem),
        scratch_shapes=[
            pltpu.VMEM((z_count, piece_rows, cols), bf16),
            pltpu.VMEM((tokens, width), bf16),
            pltpu.VMEM((4, chunk, width), bf16),
            pltpu.VMEM((4, chunk, tokens), f32),
            pltpu.SemaphoreType.DMA((9,)),
            pltpu.SemaphoreType.DMA((2, 5)),
        ],
        compiler_params=pltpu.CompilerParams(vmem_limit_bytes=56 * 2**20),
        cost_estimate=pl.CostEstimate(
            flops=4 * count * tokens * width,
            bytes_accessed=4 * count * width,
            transcendentals=4 * count * tokens,
        ),
    )(gain, *blocks, own_head, other_head)


def teacher_kernel(
    rows, own_head, other_head, own_tanh, other_tanh, student_sum, own_exp, other_exp, sums
):
    total = jnp.zeros((1, rows.shape[0]), f32)
    mixed = jnp.zeros((1, rows.shape[0]), f32)
    for head, tanh, out in ((own_head, own_tanh, own_exp), (other_head, other_tanh, other_exp)):
        logit = softcap * jnp.tanh(dot_t(rows[...], head[...]).T * (1.0 / softcap))
        grown = jnp.exp(logit)
        out[...] = grown
        total += jnp.sum(grown, axis=0, keepdims=True)
        mixed += jnp.sum(grown * (logit - softcap * tanh[...]), axis=0, keepdims=True)
    pieces = [
        row[:, i : i + 128]
        for row in (total, mixed, student_sum[...])
        for i in range(0, row.shape[1], 128)
    ]
    sums[...] = jnp.broadcast_to(jnp.concatenate(pieces, axis=0)[None], sums.shape)


def teacher_logits(rows, own_head, other_head, own_tanh, other_tanh, student_sum, plane):
    count, width = own_head.shape
    tokens = rows.shape[0]
    vmem = pl.BlockSpec(memory_space=pltpu.VMEM)
    return pl.pallas_call(
        teacher_kernel,
        out_shape=(
            jax.ShapeDtypeStruct((count, tokens), f32),
            jax.ShapeDtypeStruct((count, tokens), f32),
            jax.ShapeDtypeStruct((plane, 3 * tokens // 128, 128), f32),
        ),
        in_specs=[vmem] * 6,
        out_specs=(vmem, vmem, vmem),
        compiler_params=pltpu.CompilerParams(vmem_limit_bytes=12 * 2**20),
        cost_estimate=pl.CostEstimate(
            flops=4 * count * tokens * width,
            bytes_accessed=4 * count * width,
            transcendentals=4 * count * tokens,
        ),
    )(rows, own_head, other_head, own_tanh, other_tanh, student_sum)


def gradient_kernel(
    own_exp, other_exp, own_tanh, other_tanh, sums, weight, own_head, other_head,
    own_grad, other_grad, terms, held, turned, sem,
):
    count = own_exp.shape[0]
    chunks, _, block = held.shape
    copies = []
    for i in range(chunks):
        columns = pl.ds(i * block, block)
        for j, head in enumerate((own_head, other_head)):
            copies.append(
                pltpu.make_async_copy(
                    head.at[:, columns], held.at[i, pl.ds(j * count, count)], sem.at[i, j]
                )
            )
            copies[-1].start()
    totals = jnp.sum(sums[...], axis=0)
    each = totals.shape[0] // 3
    teacher_total = jnp.concatenate([totals[k : k + 1] for k in range(each)], axis=1)
    student_total = jnp.concatenate([totals[k : k + 1] for k in range(2 * each, 3 * each)], axis=1)
    student_factor = weight[...] / student_total
    teacher_factor = weight[...] / teacher_total
    for start, exps, tanhs, grads in (
        (0, own_exp, own_tanh, own_grad),
        (count, other_exp, other_tanh, other_grad),
    ):
        student = tanhs[...]
        grad = (jnp.exp(softcap * student) * student_factor - exps[...] * teacher_factor) * (
            1.0 - student * student
        )
        grads[...] = grad.astype(bf16)
        turned[:, pl.ds(start, count)] = grad.T.astype(bf16)
    for i in range(chunks):
        copies[2 * i].wait()
        copies[2 * i + 1].wait()
        terms[:, pl.ds(i * block, block)] = jnp.dot(
            turned[...], held[i], preferred_element_type=f32
        ).astype(bf16)


def gradient_terms(own_exp, other_exp, own_tanh, other_tanh, sums, weight, own_head, other_head):
    count, tokens = own_exp.shape
    width = own_head.shape[1]
    block = 512
    vmem = pl.BlockSpec(memory_space=pltpu.VMEM)
    anywhere = pl.BlockSpec(memory_space=pl.ANY)
    return pl.pallas_call(
        gradient_kernel,
        out_shape=(
            jax.ShapeDtypeStruct((count, tokens), bf16),
            jax.ShapeDtypeStruct((count, tokens), bf16),
            jax.ShapeDtypeStruct((tokens, width), bf16),
        ),
        in_specs=[vmem] * 6 + [anywhere] * 2,
        out_specs=(vmem, vmem, vmem),
        scratch_shapes=[
            pltpu.VMEM((width // block, 2 * count, block), bf16),
            pltpu.VMEM((tokens, 2 * count), bf16),
            pltpu.SemaphoreType.DMA((width // block, 2)),
        ],
        compiler_params=pltpu.CompilerParams(vmem_limit_bytes=56 * 2**20),
        cost_estimate=pl.CostEstimate(
            flops=4 * count * tokens * width,
            bytes_accessed=4 * count * width + 20 * count * tokens,
            transcendentals=2 * count * tokens,
        ),
    )(own_exp, other_exp, own_tanh, other_tanh, sums, weight, own_head, other_head)


def reduced_kernel(parts, normed, out):
    total = parts[0].astype(f32)
    for i in range(1, parts.shape[0]):
        total += parts[i].astype(f32)
    inner = jnp.sum(normed[...].astype(f32) * total, axis=1, keepdims=True)
    high = inner.astype(bf16).astype(f32)
    count, rows, width = out.shape
    cols = total.shape[1] // count
    lane = lax.broadcasted_iota(jnp.int32, (rows, width - cols), 1)
    behind = jnp.where(lane == 0, high, jnp.where(lane == 1, inner - high, 0.0))
    for i in range(count):
        piece = jnp.concatenate([total[:, i * cols : (i + 1) * cols], behind], axis=1)
        out[i] = piece.astype(bf16)


def reduced_pieces(parts, normed, count, width):
    rows = normed.shape[0]
    vmem = pl.BlockSpec(memory_space=pltpu.VMEM)
    return pl.pallas_call(
        reduced_kernel,
        out_shape=jax.ShapeDtypeStruct((count, rows, width), bf16),
        in_specs=[vmem, vmem],
        out_specs=vmem,
        compiler_params=pltpu.CompilerParams(vmem_limit_bytes=56 * 2**20),
        cost_estimate=pl.CostEstimate(
            flops=parts.size, bytes_accessed=2 * parts.size, transcendentals=0
        ),
    )(parts, normed)


def local(
    context,
    residual_in,
    out_proj,
    post_gain,
    final_gain,
    teacher_head,
    student_hidden,
    student_gain,
    student_head,
    kl_weight,
):
    voc_count = lax.axis_size(VOC)
    row_count = lax.axis_size(ROW)
    rows = context.shape[0]
    teacher_cols = residual_in.shape[1]
    student_cols = student_hidden.shape[1]
    teacher_width = teacher_cols * voc_count
    student_width = student_cols * voc_count
    own = rows // voc_count
    half = rows * row_count
    voc_index = lax.axis_index(VOC)
    row_index = lax.axis_index(ROW)
    half_start = lax.axis_index("c") * half

    teacher_other = swap(teacher_head)
    student_other = swap(student_head)

    pieces = spread(student_hidden, XY).reshape(-1, student_cols)

    partial = jnp.dot(context, out_proj, preferred_element_type=f32).astype(bf16)
    raw_student = student_hidden.astype(f32)
    gains = jnp.stack(halves(jnp.concatenate([post_gain, final_gain])))
    sent = jnp.concatenate(
        [
            partial.reshape(voc_count, own, teacher_width),
            residual_in.reshape(voc_count, own, teacher_cols),
            jnp.broadcast_to(gains[None], (voc_count, *gains.shape)),
        ],
        axis=2,
    )
    right, left = ring_step(pieces, pieces)
    got = lax.all_to_all(sent, VOC, 0, 0)
    teacher_rows = own_rows(got, teacher_width, teacher_cols)
    ring = [pieces, right, left]
    teacher_rows, right, left = lax.optimization_barrier((teacher_rows, right, left))
    teacher_rows = lax.all_to_all(teacher_rows, VOC, 0, 0).reshape(rows, teacher_width)
    teacher_rows, right, left = lax.optimization_barrier((teacher_rows, right, left))
    right, left = ring_step(right, left)
    ring += [right, left]
    right, left = ring_step(right, left)
    ring += [right, left]
    cut = pieces.shape[0] // 2
    right, left = ring_step(right[:cut], left[cut:])
    ring += [right, left]
    teacher_all = spread(teacher_rows, ROW).reshape(half, teacher_width)

    student_all, student_scale, tanh_mine, tanh_others, student_sum = student_logits(
        rows, student_gain[None], ring, student_head, student_other
    )
    own_scale = lax.dynamic_slice_in_dim(student_scale[:, 0], row_index * rows, rows)
    exp_mine, exp_others, sums = teacher_logits(
        teacher_all,
        teacher_head,
        teacher_other,
        tanh_mine,
        tanh_others,
        student_sum,
        lax.axis_size(PLANE),
    )
    sums, student_tied = lax.optimization_barrier((sums, student_all))
    student_all_other = swap(student_tied)
    sums = lax.all_to_all(sums, PLANE, 0, 0)
    totals = jnp.sum(sums, axis=0).reshape(3, half)
    teacher_total, mixed, student_total = totals[0], totals[1], totals[2]
    token_kl = mixed / teacher_total + jnp.log(student_total) - jnp.log(teacher_total)
    token_kl = lax.dynamic_slice_in_dim(token_kl, row_index * rows + voc_index * own, own)
    weight = lax.dynamic_slice_in_dim(kl_weight, half_start, half)

    grad_mine, grad_others, terms = gradient_terms(
        exp_mine, exp_others, tanh_mine, tanh_others, sums, weight[None], student_head, student_other
    )
    grad_back = swap(grad_others)
    parts = lax.all_to_all(terms.reshape(row_count, rows, student_width), ROW, 0, 0)
    grad_head = (
        jnp.dot(grad_mine, student_all, preferred_element_type=f32)
        + jnp.dot(grad_back, student_all_other, preferred_element_type=f32)
    ).astype(bf16)
    own_normed = lax.dynamic_slice_in_dim(student_all, row_index * rows, rows)
    last = reduced_pieces(parts, own_normed, voc_count, 256)
    last = jnp.sum(lax.all_to_all(last, VOC, 0, 0).astype(f32), axis=0)
    grad_normed = last[:, :student_cols]
    inner_total = (last[:, student_cols] + last[:, student_cols + 1]) / own_scale
    gain_piece = lax.dynamic_slice_in_dim(student_gain, voc_index * student_cols, student_cols)
    cubed = own_scale * own_scale * own_scale
    grad_hidden = (
        own_scale[:, None] * gain_piece * grad_normed
        - raw_student * cubed[:, None] * inner_total[:, None] / student_width
    ).astype(bf16)
    return (token_kl, grad_hidden, grad_head)


def solution(mesh):
    sec, tok, voc = mesh.devices.shape
    fine = Mesh(mesh.devices.reshape(sec, tok // 2, 2, 2, voc // 2), ("c", "x", "yl", "yh", "z"))
    row = ("c", "x", "yl")
    every = ("c", "x", "yl", "yh", "z")
    return jax.shard_map(
        local,
        mesh=fine,
        in_specs=(
            P(row, VOC),
            P(row, VOC),
            P(VOC, None),
            P(VOC),
            P(VOC),
            P(every, None),
            P(row, VOC),
            P(),
            P(every, None),
            P(),
        ),
        out_specs=(P(every), P(row, VOC), P(every, None)),
        check_vma=False,
    )
```
